32 devices in a mesh: tm: 8 (over z, core), head: 4 (over y, x).
Axes of the slice: x: 2, y: 2, z: 4, core: 2. Of those that a mesh axis runs over, the one named last changes fastest.
Arguments:
- query: bfloat16 [10240, 12, 128], P(('tm', 'head')), may hold values from -15 to 15
- key: bfloat16 [10240, 12, 128], P(('tm', 'head')), may hold values from -15 to 15
- value: bfloat16 [10240, 12, 128], P(('tm', 'head')), may hold values from -6 to 6
- far_list: int32 [80, 8], P('tm'), may hold values from 0 to 79, as said below
- far_count: int32 [80, 8], P('tm'), may hold values from 0 to 1, as said below
Outputs:
- attended: bfloat16 [10240, 12, 128], P(('tm', 'head'))
The draws below stay inside these ranges and needn't reach their ends.
Inputs may be any that keep to these rules, and one draw needn't show every extreme that they name: far_list[b, g] is a block of frame g: far_list[b, g] // 10 == g. far_count[b, g] is 0 where the frame of block b and frame g are less than 2 apart. For frames f and g at distance d >= 2, exactly min(5, max(1, 2, 2 * 5 // d)) of the 10 blocks of frame f have far_count 1 for g; so at most 5 blocks of a frame list blocks of one other frame, and exactly 5 at distance 2.
All inputs are finite; a program needn't handle non-finite values.
Results may differ from the reference program's by a relative error of at most 0.012.
Values may be sent and summed in bfloat16 or wider, within the bound.
A program may use at most 128 MiB of HBM per device.

```python
import jax
import jax.numpy as jnp
from jax import lax

FW = 80
BLK = 128
DH = 128
RT = 16
RH = 56
RW = 56
HEADS = 12
FRAME_TOK = 1280
FRAMES = 8
TOKENS = 10240
BLOCKS = 80
FRAME_BLOCKS = 10
CAP = 5


def loose_rows(key, spread, salt):
    fresh = jax.random.fold_in(key, salt)
    return jnp.clip(jax.random.normal(fresh, (TOKENS, HEADS, DH), jnp.float32) * spread, -15.0, 15.0)


def draw_query(key, part):
    drawn = loose_rows(key, 2.5, 1)
    return drawn.astype(jnp.bfloat16)


def draw_key(key, part):
    drawn = loose_rows(key, 1.0, 2)
    return drawn.astype(jnp.bfloat16)


def one_permutation(pair_key):
    return jax.random.permutation(pair_key, FRAME_BLOCKS)


def mask_tables(key):
    salt = jax.random.fold_in(key, 777)
    block_frame = jnp.arange(BLOCKS) // FRAME_BLOCKS
    source = jnp.arange(FRAMES)
    frame_gap = jnp.abs(block_frame[:, None] - source[None, :])
    quota = jnp.minimum(CAP, jnp.maximum(jnp.maximum(1, 2 * CAP // 5), 2 * CAP // jnp.maximum(frame_gap, 1)))
    pair_keys = jax.random.split(jax.random.fold_in(salt, 1), FRAMES * FRAMES)
    ranks = jax.vmap(one_permutation)(pair_keys)
    ranks = ranks.reshape(FRAMES, FRAMES, FRAME_BLOCKS).transpose(0, 2, 1).reshape(BLOCKS, FRAMES)
    listed = ((frame_gap >= 2) & (ranks < quota)).astype(jnp.int32)
    local_ids = jax.random.randint(jax.random.fold_in(salt, 2), (BLOCKS, FRAMES), 0, FRAME_BLOCKS)
    return ((source[None, :] * FRAME_BLOCKS + local_ids).astype(jnp.int32), listed)


def draw_far_list(key, part):
    return mask_tables(key)[0]


def draw_far_count(key, part):
    return mask_tables(key)[1]


def block_levels(own_key, shape, shards, smallest, high):
    level, own = 1.0, jax.random.fold_in(own_key, 6)
    for position, shards_of in shards:
        steps = jnp.exp(jax.random.uniform(jax.random.fold_in(own, position), (shards_of,), jnp.float32, smallest / len(shards), high / len(shards)))
        level = level * jnp.repeat(steps, shape[position] // shards_of).reshape([-1 if axis == position else 1 for axis in range(len(shape))])
    return level


def bell_draw(own_key, extent, scale, bound, cuts=(), kind=jnp.bfloat16):
    entries = jax.random.normal(own_key, extent, jnp.float32) * scale
    if len(cuts) > 0:
        entries = block_levels(own_key, extent, cuts, -0.22, 0.18) * entries
    return jnp.clip(entries, min=-bound, max=bound).astype(kind)


def setup_inputs(seed: int = 0) -> dict:
    arg_keys = jax.random.split(jax.random.key(seed), 6)
    query = draw_query(jax.random.fold_in(arg_keys[5], 71), 0)
    key = draw_key(jax.random.fold_in(arg_keys[5], 71), 0)
    value = bell_draw(arg_keys[2], (TOKENS, HEADS, DH), 1.0, 6.0, ((0, 32),))
    far_list = draw_far_list(jax.random.fold_in(arg_keys[5], 71), 0)
    far_count = draw_far_count(jax.random.fold_in(arg_keys[5], 71), 0)
    return dict(query=query, key=key, value=value, far_list=far_list, far_count=far_count)


THETA = 256.0


def swap_matrix(head_width):
    row_ids = jnp.arange(head_width)[:, None]
    col_ids = jnp.arange(head_width)[None, :]
    minus_one = (row_ids == col_ids + 1) & (col_ids % 2 == 0)
    plus_one = (col_ids == row_ids + 1) & (row_ids % 2 == 0)
    return jnp.where(plus_one, 1.0, jnp.where(minus_one, -1.0, 0.0)).astype(jnp.bfloat16)


def axis_angles(positions, span_width):
    pair_index = jnp.arange(span_width // 2).astype(jnp.float32)
    inverse = THETA ** (-2.0 * pair_index / span_width)
    return positions[:, None] * inverse[None, :]


def rotate(values, frame_pos, row_pos, col_pos):
    token_count, head_count, head_width = values.shape
    angles = jnp.concatenate([axis_angles(frame_pos, RT), axis_angles(row_pos, RH), axis_angles(col_pos, RW)], axis=1)
    angles = jnp.repeat(angles, 2, axis=1)
    swapped = jnp.dot(values.reshape(token_count * head_count, head_width), swap_matrix(head_width), preferred_element_type=jnp.float32)
    swapped = swapped.reshape(token_count, head_count, head_width)
    turned = values.astype(jnp.float32) * jnp.cos(angles)[:, None, :] + swapped * jnp.sin(angles)[:, None, :]
    return turned.astype(jnp.bfloat16)


def reference(query, key, value, far_list, far_count):
    token_index = jnp.arange(TOKENS, dtype=jnp.int32)
    frame_pos = (token_index // FRAME_TOK).astype(jnp.float32)
    row_pos = ((token_index % FRAME_TOK) // FW).astype(jnp.float32)
    col_pos = (token_index % FW).astype(jnp.float32)
    turned_q = lax.optimization_barrier(jnp.transpose(rotate(query, frame_pos, row_pos, col_pos), (1, 0, 2)))
    turned_k = lax.optimization_barrier(jnp.transpose(rotate(key, frame_pos, row_pos, col_pos), (1, 0, 2)))
    values_t = jnp.transpose(value, (1, 0, 2))
    score_scale = DH ** -0.5
    padded_k = jnp.pad(turned_k, ((0, 0), (FRAME_TOK, FRAME_TOK), (0, 0)))
    padded_v = jnp.pad(values_t, ((0, 0), (FRAME_TOK, FRAME_TOK), (0, 0)))
    key_blocks = turned_k.reshape(HEADS, BLOCKS, BLK, DH)
    value_blocks = values_t.reshape(HEADS, BLOCKS, BLK, DH)

    def one_block(block):
        frame_index = (block // FRAME_BLOCKS).astype(jnp.int32)
        query_rows = lax.dynamic_slice_in_dim(turned_q, (block * BLK).astype(jnp.int32), BLK, 1)
        near_keys = lax.dynamic_slice_in_dim(padded_k, (frame_index * FRAME_TOK).astype(jnp.int32), 3 * FRAME_TOK, 1)
        near_values = lax.dynamic_slice_in_dim(padded_v, (frame_index * FRAME_TOK).astype(jnp.int32), 3 * FRAME_TOK, 1)
        key_frame = jnp.arange(3 * FRAME_TOK, dtype=jnp.int32) // FRAME_TOK + frame_index - 1
        near_ok = (key_frame >= 0) & (key_frame < FRAMES)
        far_ids = far_list[block].astype(jnp.int32)
        far_keys = jnp.take(key_blocks, far_ids, axis=1).reshape(HEADS, FRAMES * BLK, DH)
        far_values = jnp.take(value_blocks, far_ids, axis=1).reshape(HEADS, FRAMES * BLK, DH)
        far_ok = jnp.repeat(far_count[block] > 0, BLK)
        keys_all = jnp.concatenate([near_keys, far_keys], axis=1)
        values_all = jnp.concatenate([near_values, far_values], axis=1)
        valid = jnp.concatenate([near_ok, far_ok], axis=0)
        scores = jnp.einsum("hid,hjd->hij", query_rows.astype(jnp.float32), keys_all.astype(jnp.float32)) * score_scale
        scores = jnp.where(valid[None, None, :], scores, -jnp.inf)
        row_max = jnp.max(scores, axis=2)
        weights = jnp.exp(scores - row_max[..., None])
        row_total = jnp.sum(weights, axis=2)
        rounded = lax.optimization_barrier(weights.astype(jnp.bfloat16))
        mixed = jnp.einsum("hij,hjd->hid", rounded.astype(jnp.float32), values_all.astype(jnp.float32))
        return (mixed / row_total[..., None]).astype(jnp.bfloat16)

    attended = lax.map(one_block, jnp.arange(BLOCKS, dtype=jnp.int32))
    return jnp.transpose(attended, (0, 2, 1, 3)).reshape(TOKENS, HEADS, DH)
```

```python
import functools

import jax
import jax.numpy as jnp
from jax import lax
from jax.experimental import pallas as pl
from jax.experimental.pallas import tpu as pltpu
from jax.sharding import PartitionSpec as P

FW = 80
BLK = 128
RT = 16
RH = 56
RW = 56
CAP = 5
THETA = 256.0
MESH = pl.DeviceIdType.MESH


def quota(gap):
    return min(CAP, max(1, 2 * CAP // 5, 2 * CAP // gap))


def slot_layout(frames):
    sizes = [0] * frames
    for offset in range(1, frames):
        sizes[offset] = max([quota(d) for d in (offset, frames - offset) if d >= 2])
    starts, total = [0] * frames, 0
    for offset in range(1, frames):
        starts[offset] = total
        total += sizes[offset]
    return sizes, starts, total


def swap_matrix(head_width):
    row_ids = jnp.arange(head_width)[:, None]
    col_ids = jnp.arange(head_width)[None, :]
    minus_one = (row_ids == col_ids + 1) & (col_ids % 2 == 0)
    plus_one = (col_ids == row_ids + 1) & (row_ids % 2 == 0)
    return jnp.where(plus_one, 1.0, jnp.where(minus_one, -1.0, 0.0)).astype(jnp.bfloat16)


def axis_angles(positions, span_width):
    pair_index = jnp.arange(span_width // 2).astype(jnp.float32)
    inverse = THETA ** (-2.0 * pair_index / span_width)
    return positions[:, None] * inverse[None, :]


def kernel(
    frames, groups, own_heads, frame_tok, width,
    pick_ref, q_in, k_in, v_in, cos_ref, sin_ref, swap_ref, bias_ref, out_ref,
    *scratch,
):
    sizes, starts, slots = slot_layout(frames)
    span = frame_tok // groups
    blocks = frame_tok // BLK
    own, lo, hi, far = (
        scratch[i * own_heads : (i + 1) * own_heads] for i in range(4)
    )
    (
        q_own, rot_q, rot_k, sent, done,
        in_send, in_recv, in_local, halo_send, halo_recv, far_send, far_recv,
        out_send, out_recv, out_local,
    ) = scratch[4 * own_heads :]
    rings = sent.shape[0]
    frame = lax.axis_index("tm")
    group = lax.axis_index("head")

    for h in range(own_heads):
        far[h][...] = jnp.zeros_like(far[h])

    @pl.when(frame == 0)
    def _():
        for h in range(own_heads):
            lo[h][...] = jnp.zeros_like(lo[h])

    @pl.when(frame == frames - 1)
    def _():
        for h in range(own_heads):
            hi[h][...] = jnp.zeros_like(hi[h])

    barrier = pltpu.get_barrier_semaphore()
    for step in range(1, groups):
        pl.semaphore_signal(
            barrier, inc=1, device_id=(frame, lax.rem(group + step, groups)), device_id_type=MESH
        )
    for step in range(1, frames):
        pl.semaphore_signal(
            barrier, inc=1, device_id=(lax.rem(frame + step, frames), group), device_id_type=MESH
        )
    pl.semaphore_wait(barrier, groups + frames - 2)

    def landing(which, h, source):
        rows = pl.ds(pl.multiple_of(source * span, span), span)
        return q_own.at[h, rows] if which == 2 else own[h].at[which, rows]

    def in_copy(which, h, step):
        peer = lax.rem(group + step, groups)
        source = (rot_k, v_in, rot_q)[which]
        return pltpu.make_async_remote_copy(
            src_ref=source.at[peer * own_heads + h],
            dst_ref=landing(which, h, group),
            send_sem=in_send.at[which, h, step - 1],
            recv_sem=in_recv.at[which, h, step - 1],
            device_id=(frame, peer),
            device_id_type=MESH,
        )

    def in_own(which, h):
        source = (rot_k, v_in, rot_q)[which]
        return pltpu.make_async_copy(
            source.at[group * own_heads + h], landing(which, h, group), in_local.at[which, h]
        )

    def rotate_head(source, target, head):
        x = source[head]
        swapped = jnp.dot(x, swap_ref[...], preferred_element_type=jnp.float32)
        turned = x.astype(jnp.float32) * cos_ref[...] + swapped * sin_ref[...]
        target[head] = turned.astype(jnp.bfloat16)

    for h in range(own_heads):
        for which, (source, target) in ((1, (None, None)), (0, (k_in, rot_k)), (2, (q_in, rot_q))):
            if source is not None:
                for step in range(groups):
                    rotate_head(source, target, step * own_heads + h)
            for step in range(1, groups):
                in_copy(which, h, step).start()
            in_own(which, h).start()

    def in_wait(which, h):
        for step in range(1, groups):
            in_copy(which, h, step).wait_recv()
        in_own(which, h).wait()

    def halo_copy(h, up):
        peer = lax.rem(frame + (1 if up else frames - 1), frames)
        return pltpu.make_async_remote_copy(
            src_ref=own[h],
            dst_ref=(lo if up else hi)[h],
            send_sem=halo_send.at[h, int(up)],
            recv_sem=halo_recv.at[h, int(up)],
            device_id=(peer, group),
            device_id_type=MESH,
        )

    def far_copy(h, offset, count):
        place = pl.ds(starts[offset] * BLK, count * BLK)
        return pltpu.make_async_remote_copy(
            src_ref=sent.at[h % rings, :, place],
            dst_ref=far[h].at[:, place],
            send_sem=far_send.at[h, offset - 1],
            recv_sem=far_recv.at[h, offset - 1],
            device_id=(lax.rem(frame + frames - offset, frames), group),
            device_id_type=MESH,
        )

    def each_far(straight, action, h):
        for offset in range(1, frames):
            direct = straight(offset)
            for condition, gap in ((direct, offset), (jnp.logical_not(direct), frames - offset)):
                if gap >= 2:

                    @pl.when(condition)
                    def _(offset=offset, gap=gap):
                        action(far_copy(h, offset, quota(gap)))

    def sends_far(action, h):
        each_far(lambda offset: frame >= offset, action, h)

    def takes_far(action, h):
        each_far(lambda offset: frame + offset < frames, action, h)

    def sends_halo(action, h):
        @pl.when(frame < frames - 1)
        def _():
            action(halo_copy(h, True))

        @pl.when(frame > 0)
        def _():
            action(halo_copy(h, False))

    def takes_halo(action, h):
        @pl.when(frame > 0)
        def _():
            action(halo_copy(h, True))

        @pl.when(frame < frames - 1)
        def _():
            action(halo_copy(h, False))

    def begin(copy):
        copy.start()

    def wait_send(copy):
        copy.wait_send()

    def wait_recv(copy):
        copy.wait_recv()

    def spread(h):
        in_wait(1, h)
        in_wait(0, h)
        sends_halo(begin, h)
        if h >= rings:
            sends_far(wait_send, h - rings)

        def pick(slot, carry):
            found = jnp.zeros((2, BLK // 16, 16, width), jnp.bfloat16)
            for block in range(blocks):
                part = own[h][:, block * BLK : (block + 1) * BLK, :]
                found = found + part.reshape(found.shape) * pick_ref[slot, block]
            rows = pl.ds(pl.multiple_of(slot * BLK, BLK), BLK)
            sent[h % rings, :, rows, :] = found.reshape(2, BLK, width)
            return carry

        lax.fori_loop(0, slots, pick, 0)
        sends_far(begin, h)

    scale = (width ** -0.5) * 1.4426950408889634
    tile = 2 * BLK
    low_bias = jnp.where(frame > 0, 0.0, -jnp.inf)
    high_bias = jnp.where(frame < frames - 1, 0.0, -jnp.inf)

    def score(rows, keys):
        return lax.dot_general(
            rows, keys, (((1,), (1,)), ((), ())), preferred_element_type=jnp.float32
        )

    def attend(h):
        def one_tile(index, carry):
            rows = q_own[h, pl.ds(pl.multiple_of(index * tile, tile), tile), :]
            near = [
                score(rows, lo[h][0]) + low_bias,
                score(rows, own[h][0]),
                score(rows, hi[h][0]) + high_bias,
            ]
            tops = [jnp.max(part, axis=1, keepdims=True) for part in near]
            top = jnp.maximum(jnp.maximum(tops[0], tops[1]), tops[2])
            found = score(rows, far[h][0]).reshape(2, BLK, slots * BLK)
            found = found + bias_ref[pl.ds(index * 2, 2)]
            found = found.reshape(tile, slots * BLK)
            top = jnp.maximum(top, jnp.max(found, axis=1, keepdims=True))
            total = jnp.zeros((tile, 1), jnp.float32)
            summed = jnp.zeros((tile, width), jnp.float32)
            for part, values in zip(near + [found], (lo[h], own[h], hi[h], far[h])):
                weights = jnp.exp2((part - top) * scale)
                total = total + jnp.sum(weights, axis=1, keepdims=True)
                summed = summed + jnp.dot(
                    weights.astype(jnp.bfloat16), values[1], preferred_element_type=jnp.float32
                )
            done[h, pl.ds(pl.multiple_of(index * tile, tile), tile), :] = (
                summed / total
            ).astype(jnp.bfloat16)
            return carry

        lax.fori_loop(0, frame_tok // tile, one_tile, 0)

    def out_copy(h, step):
        peer = lax.rem(group + step, groups)
        return pltpu.make_async_remote_copy(
            src_ref=done.at[h, pl.ds(pl.multiple_of(peer * span, span), span)],
            dst_ref=out_ref.at[group * own_heads + h],
            send_sem=out_send.at[h, step - 1],
            recv_sem=out_recv.at[h, step - 1],
            device_id=(frame, peer),
            device_id_type=MESH,
        )

    def out_own(h):
        return pltpu.make_async_copy(
            done.at[h, pl.ds(pl.multiple_of(group * span, span), span)],
            out_ref.at[group * own_heads + h],
            out_local.at[h],
        )

    spread(0)
    if own_heads > 1:
        spread(1)
    for h in range(own_heads):
        in_wait(2, h)
        takes_halo(wait_recv, h)
        takes_far(wait_recv, h)
        if h + 2 < own_heads:
            spread(h + 2)
        attend(h)
        for step in range(1, groups):
            out_copy(h, step).start()
        out_own(h).start()

    for h in range(own_heads):
        for which in range(3):
            for step in range(1, groups):
                in_copy(which, h, step).wait_send()
        sends_halo(wait_send, h)
        if h + rings >= own_heads:
            sends_far(wait_send, h)
        for step in range(1, groups):
            out_copy(h, step).wait()
        out_own(h).wait()


def shards(query, key, value, far_list, far_count):
    frames = lax.axis_size("tm")
    groups = lax.axis_size("head")
    frame = lax.axis_index("tm")
    group = lax.axis_index("head")
    span, heads, width = query.shape
    own_heads = heads // groups
    frame_tok = span * groups
    blocks = frame_tok // BLK
    sizes, starts, slots = slot_layout(frames)

    local_ids = jnp.clip(far_list - jnp.arange(frames)[None, :] * blocks, 0, blocks - 1)
    wanted = far_count > 0
    rank = jnp.cumsum(wanted.astype(jnp.int32), axis=0) - 1
    picks = jnp.arange(CAP)[:, None, None]
    asked = jnp.sum(
        jnp.where(wanted[None] & (rank[None] == picks), local_ids[None], 0), axis=1
    ).astype(jnp.int32)
    heard = lax.all_to_all(
        jnp.transpose(asked, (1, 0)), "tm", split_axis=0, concat_axis=0, tiled=True
    )
    offset_of = jnp.array([o for o in range(1, frames) for _ in range(sizes[o])], jnp.int32)
    pick_of = jnp.array([i for o in range(1, frames) for i in range(sizes[o])], jnp.int32)
    requests = heard[(frame - offset_of) % frames, pick_of]
    offsets = jnp.arange(1, frames)
    source = (frame + offsets) % frames
    there = jnp.take(wanted, source, axis=1)
    place = jnp.take(rank, source, axis=1)
    bias = jnp.concatenate(
        [
            jnp.where(
                there[:, o - 1, None] & (place[:, o - 1, None] == jnp.arange(sizes[o])[None, :]),
                0.0,
                -jnp.inf,
            )
            for o in range(1, frames)
        ],
        axis=1,
    ).astype(jnp.float32)
    bias = jnp.repeat(bias, BLK, axis=1)[:, None, :]
    picked = requests[:, None] == jnp.arange(blocks)[None, :]
    picked = jnp.broadcast_to(
        picked.astype(jnp.bfloat16)[:, :, None, None], (slots, blocks, 16, width)
    )

    token = group * span + jnp.arange(span)
    angles = jnp.concatenate(
        [
            axis_angles(jnp.zeros((span,), jnp.float32) + frame.astype(jnp.float32), RT),
            axis_angles((token // FW).astype(jnp.float32), RH),
            axis_angles((token % FW).astype(jnp.float32), RW),
        ],
        axis=1,
    )
    cosines = jnp.repeat(jnp.cos(angles), 2, axis=1)
    sines = jnp.repeat(jnp.sin(angles), 2, axis=1)

    rings = min(own_heads, 3)
    bf16 = jnp.bfloat16
    whole_frame = pltpu.VMEM((2, frame_tok, width), bf16)
    dma = pltpu.SemaphoreType.DMA
    vmem = pl.BlockSpec(memory_space=pltpu.VMEM)
    anywhere = pl.BlockSpec(memory_space=pl.ANY)
    keys_seen = 3 * frame_tok + slots * BLK
    attended = pl.pallas_call(
        functools.partial(kernel, frames, groups, own_heads, frame_tok, width),
        out_shape=jax.ShapeDtypeStruct((heads, span, width), bf16),
        in_specs=[vmem, vmem, vmem, anywhere, vmem, vmem, vmem, vmem],
        out_specs=anywhere,
        scratch_shapes=[whole_frame] * (3 * own_heads)
        + [pltpu.VMEM((2, slots * BLK, width), bf16)] * own_heads
        + [
            pltpu.VMEM((own_heads, frame_tok, width), bf16),
            pltpu.VMEM((heads, span, width), bf16),
            pltpu.VMEM((heads, span, width), bf16),
            pltpu.VMEM((rings, 2, slots * BLK, width), bf16),
            pltpu.VMEM((own_heads, frame_tok, width), bf16),
            dma((3, own_heads, groups - 1)),
            dma((3, own_heads, groups - 1)),
            dma((3, own_heads)),
            dma((own_heads, 2)),
            dma((own_heads, 2)),
            dma((own_heads, frames - 1)),
            dma((own_heads, frames - 1)),
            dma((own_heads, groups - 1)),
            dma((own_heads, groups - 1)),
            dma((own_heads,)),
        ],
        compiler_params=pltpu.CompilerParams(
            collective_id=0, has_side_effects=True, vmem_limit_bytes=62 * 1024 * 1024
        ),
        cost_estimate=pl.CostEstimate(
            flops=4 * own_heads * frame_tok * keys_seen * width,
            bytes_accessed=8 * heads * span * width,
            transcendentals=own_heads * frame_tok * keys_seen,
        ),
    )(
        picked,
        jnp.transpose(query, (1, 0, 2)),
        jnp.transpose(key, (1, 0, 2)),
        jnp.transpose(value, (1, 0, 2)),
        cosines,
        sines,
        swap_matrix(width),
        bias,
    )
    return jnp.transpose(attended, (1, 0, 2))


def solution(mesh):
    in_specs = (
        P(("tm", "head"), None, None),
        P(("tm", "head"), None, None),
        P(("tm", "head"), None, None),
        P("tm", None),
        P("tm", None),
    )
    out_specs = P(("tm", "head"), None, None)
    return jax.shard_map(shards, mesh=mesh, in_specs=in_specs, out_specs=out_specs, check_vma=False)
```

```python
import functools

import jax
import jax.numpy as jnp
from jax import lax
from jax.experimental import pallas as pl
from jax.experimental.pallas import tpu as pltpu
from jax.sharding import PartitionSpec as P

FW = 80
BLK = 128
RT = 16
RH = 56
RW = 56
CAP = 5
THETA = 256.0
MESH = pl.DeviceIdType.MESH


def quota(gap):
    return min(CAP, max(1, 2 * CAP // 5, 2 * CAP // gap))


def slot_layout(frames):
    sizes = [0] * frames
    for offset in range(1, frames):
        sizes[offset] = max([quota(d) for d in (offset, frames - offset) if d >= 2])
    starts, total = [0] * frames, 0
    for offset in range(1, frames):
        starts[offset] = total
        total += sizes[offset]
    return sizes, starts, total


def swap_matrix(head_width):
    row_ids = jnp.arange(head_width)[:, None]
    col_ids = jnp.arange(head_width)[None, :]
    minus_one = (row_ids == col_ids + 1) & (col_ids % 2 == 0)
    plus_one = (col_ids == row_ids + 1) & (row_ids % 2 == 0)
    return jnp.where(plus_one, 1.0, jnp.where(minus_one, -1.0, 0.0)).astype(jnp.bfloat16)


def axis_angles(positions, span_width):
    pair_index = jnp.arange(span_width // 2).astype(jnp.float32)
    inverse = THETA ** (-2.0 * pair_index / span_width)
    return positions[:, None] * inverse[None, :]


def kernel(
    frames, groups, own_heads, frame_tok, width,
    pick_ref, q_in, k_in, v_in, cos_ref, sin_ref, swap_ref, bias_ref, out_ref,
    *scratch,
):
    sizes, starts, slots = slot_layout(frames)
    span = frame_tok // groups
    blocks = frame_tok // BLK
    own, lo, hi, far = (
        scratch[i * own_heads : (i + 1) * own_heads] for i in range(4)
    )
    (
        q_own, rot_q, rot_k, sent, done,
        in_send, in_recv, in_local, halo_send, halo_recv, far_send, far_recv,
        out_send, out_recv, out_local,
    ) = scratch[4 * own_heads :]
    rings = sent.shape[0]
    frame = lax.axis_index("tm")
    group = lax.axis_index("head")

    for h in range(own_heads):
        far[h][...] = jnp.zeros_like(far[h])

    @pl.when(frame == 0)
    def _():
        for h in range(own_heads):
            lo[h][...] = jnp.zeros_like(lo[h])

    @pl.when(frame == frames - 1)
    def _():
        for h in range(own_heads):
            hi[h][...] = jnp.zeros_like(hi[h])

    barrier = pltpu.get_barrier_semaphore()
    for step in range(1, groups):
        pl.semaphore_signal(
            barrier, inc=1, device_id=(frame, lax.rem(group + step, groups)), device_id_type=MESH
        )
    for step in range(1, frames):
        pl.semaphore_signal(
            barrier, inc=1, device_id=(lax.rem(frame + step, frames), group), device_id_type=MESH
        )
    pl.semaphore_wait(barrier, groups + frames - 2)

    def landing(which, h, source):
        rows = pl.ds(pl.multiple_of(source * span, span), span)
        return q_own.at[h, rows] if which == 2 else own[h].at[which, rows]

    def in_copy(which, h, step):
        peer = lax.rem(group + step, groups)
        source = (rot_k, v_in, rot_q)[which]
        return pltpu.make_async_remote_copy(
            src_ref=source.at[peer * own_heads + h],
            dst_ref=landing(which, h, group),
            send_sem=in_send.at[which, h, step - 1],
            recv_sem=in_recv.at[which, h, step - 1],
            device_id=(frame, peer),
            device_id_type=MESH,
        )

    def in_own(which, h):
        source = (rot_k, v_in, rot_q)[which]
        return pltpu.make_async_copy(
            source.at[group * own_heads + h], landing(which, h, group), in_local.at[which, h]
        )

    def rotate_head(source, target, head):
        x = source[head]
        swapped = jnp.dot(x, swap_ref[...], preferred_element_type=jnp.float32)
        turned = x.astype(jnp.float32) * cos_ref[...] + swapped * sin_ref[...]
        target[head] = turned.astype(jnp.bfloat16)

    for h in range(own_heads):
        for which, (source, target) in ((1, (None, None)), (0, (k_in, rot_k)), (2, (q_in, rot_q))):
            if source is not None:
                for step in range(groups):
                    rotate_head(source, target, step * own_heads + h)
            for step in range(1, groups):
                in_copy(which, h, step).start()
            in_own(which, h).start()

    def in_wait(which, h):
        for step in range(1, groups):
            in_copy(which, h, step).wait_recv()
        in_own(which, h).wait()

    def halo_copy(h, up):
        peer = lax.rem(frame + (1 if up else frames - 1), frames)
        return pltpu.make_async_remote_copy(
            src_ref=own[h],
            dst_ref=(lo if up else hi)[h],
            send_sem=halo_send.at[h, int(up)],
            recv_sem=halo_recv.at[h, int(up)],
            device_id=(peer, group),
            device_id_type=MESH,
        )

    def far_copy(h, offset, count):
        place = pl.ds(starts[offset] * BLK, count * BLK)
        return pltpu.make_async_remote_copy(
            src_ref=sent.at[h % rings, :, place],
            dst_ref=far[h].at[:, place],
            send_sem=far_send.at[h, offset - 1],
            recv_sem=far_recv.at[h, offset - 1],
            device_id=(lax.rem(frame + frames - offset, frames), group),
            device_id_type=MESH,
        )

    def each_far(straight, action, h):
        for offset in range(1, frames):
            direct = straight(offset)
            for condition, gap in ((direct, offset), (jnp.logical_not(direct), frames - offset)):
                if gap >= 2:

                    @pl.when(condition)
                    def _(offset=offset, gap=gap):
                        action(far_copy(h, offset, quota(gap)))

    def sends_far(action, h):
        each_far(lambda offset: frame >= offset, action, h)

    def takes_far(action, h):
        each_far(lambda offset: frame + offset < frames, action, h)

    def sends_halo(action, h):
        @pl.when(frame < frames - 1)
        def _():
            action(halo_copy(h, True))

        @pl.when(frame > 0)
        def _():
            action(halo_copy(h, False))

    def takes_halo(action, h):
        @pl.when(frame > 0)
        def _():
            action(halo_copy(h, True))

        @pl.when(frame < frames - 1)
        def _():
            action(halo_copy(h, False))

    def begin(copy):
        copy.start()

    def wait_send(copy):
        copy.wait_send()

    def wait_recv(copy):
        copy.wait_recv()

    def spread(h):
        in_wait(1, h)
        in_wait(0, h)
        sends_halo(begin, h)
        if h >= rings:
            sends_far(wait_send, h - rings)

        def pick(slot, carry):
            found = jnp.zeros((2, BLK // 16, 16, width), jnp.bfloat16)
            for block in range(blocks):
                part = own[h][:, block * BLK : (block + 1) * BLK, :]
                found = found + part.reshape(found.shape) * pick_ref[slot, block]
            rows = pl.ds(pl.multiple_of(slot * BLK, BLK), BLK)
            sent[h % rings, :, rows, :] = found.reshape(2, BLK, width)
            return carry

        lax.fori_loop(0, slots, pick, 0)
        sends_far(begin, h)

    scale = (width ** -0.5) * 1.4426950408889634
    tile = 2 * BLK
    low_bias = jnp.where(frame > 0, 0.0, -jnp.inf)
    high_bias = jnp.where(frame < frames - 1, 0.0, -jnp.inf)

    def score(rows, keys):
        return lax.dot_general(
            rows, keys, (((1,), (1,)), ((), ())), preferred_element_type=jnp.float32
        )

    def attend(h):
        def one_tile(index, carry):
            rows = q_own[h, pl.ds(pl.multiple_of(index * tile, tile), tile), :]
            near = [
                score(rows, lo[h][0]) + low_bias,
                score(rows, own[h][0]),
                score(rows, hi[h][0]) + high_bias,
            ]
            tops = [jnp.max(part, axis=1, keepdims=True) for part in near]
            top = jnp.maximum(jnp.maximum(tops[0], tops[1]), tops[2])
            found = score(rows, far[h][0]).reshape(2, BLK, slots * BLK)
            found = found + bias_ref[pl.ds(index * 2, 2)]
            found = found.reshape(tile, slots * BLK)
            top = jnp.maximum(top, jnp.max(found, axis=1, keepdims=True))
            total = jnp.zeros((tile, 1), jnp.float32)
            summed = jnp.zeros((tile, width), jnp.float32)
            for part, values in zip(near + [found], (lo[h], own[h], hi[h], far[h])):
                weights = jnp.exp2((part - top) * scale)
                total = total + jnp.sum(weights, axis=1, keepdims=True)
                summed = summed + jnp.dot(
                    weights.astype(jnp.bfloat16), values[1], preferred_element_type=jnp.float32
                )
            done[h, pl.ds(pl.multiple_of(index * tile, tile), tile), :] = (
                summed / total
            ).astype(jnp.bfloat16)
            return carry

        lax.fori_loop(0, frame_tok // tile, one_tile, 0)

    def out_copy(h, step):
        peer = lax.rem(group + step, groups)
        return pltpu.make_async_remote_copy(
            src_ref=done.at[h, pl.ds(pl.multiple_of(peer * span, span), span)],
            dst_ref=out_ref.at[group * own_heads + h],
            send_sem=out_send.at[h, step - 1],
            recv_sem=out_recv.at[h, step - 1],
            device_id=(frame, peer),
            device_id_type=MESH,
        )

    def out_own(h):
        return pltpu.make_async_copy(
            done.at[h, pl.ds(pl.multiple_of(group * span, span), span)],
            out_ref.at[group * own_heads + h],
            out_local.at[h],
        )

    for h in range(min(own_heads, 3)):
        spread(h)
    for h in range(own_heads):
        in_wait(2, h)
        takes_halo(wait_recv, h)
        takes_far(wait_recv, h)
        if h + 3 < own_heads:
            spread(h + 3)
        attend(h)
        for step in range(1, groups):
            out_copy(h, step).start()
        out_own(h).start()

    for h in range(own_heads):
        for which in range(3):
            for step in range(1, groups):
                in_copy(which, h, step).wait_send()
        sends_halo(wait_send, h)
        if h + rings >= own_heads:
            sends_far(wait_send, h)
        for step in range(1, groups):
            out_copy(h, step).wait()
        out_own(h).wait()


def shards(query, key, value, far_list, far_count):
    frames = lax.axis_size("tm")
    groups = lax.axis_size("head")
    frame = lax.axis_index("tm")
    group = lax.axis_index("head")
    span, heads, width = query.shape
    own_heads = heads // groups
    frame_tok = span * groups
    blocks = frame_tok // BLK
    sizes, starts, slots = slot_layout(frames)

    local_ids = jnp.clip(far_list - jnp.arange(frames)[None, :] * blocks, 0, blocks - 1)
    wanted = far_count > 0
    rank = jnp.cumsum(wanted.astype(jnp.int32), axis=0) - 1
    picks = jnp.arange(CAP)[:, None, None]
    asked = jnp.sum(
        jnp.where(wanted[None] & (rank[None] == picks), local_ids[None], 0), axis=1
    ).astype(jnp.int32)
    heard = lax.all_to_all(
        jnp.transpose(asked, (1, 0)), "tm", split_axis=0, concat_axis=0, tiled=True
    )
    offset_of = jnp.array([o for o in range(1, frames) for _ in range(sizes[o])], jnp.int32)
    pick_of = jnp.array([i for o in range(1, frames) for i in range(sizes[o])], jnp.int32)
    requests = heard[(frame - offset_of) % frames, pick_of]
    offsets = jnp.arange(1, frames)
    source = (frame + offsets) % frames
    there = jnp.take(wanted, source, axis=1)
    place = jnp.take(rank, source, axis=1)
    bias = jnp.concatenate(
        [
            jnp.where(
                there[:, o - 1, None] & (place[:, o - 1, None] == jnp.arange(sizes[o])[None, :]),
                0.0,
                -jnp.inf,
            )
            for o in range(1, frames)
        ],
        axis=1,
    ).astype(jnp.float32)
    bias = jnp.repeat(bias, BLK, axis=1)[:, None, :]
    picked = requests[:, None] == jnp.arange(blocks)[None, :]
    picked = jnp.broadcast_to(
        picked.astype(jnp.bfloat16)[:, :, None, None], (slots, blocks, 16, width)
    )

    token = group * span + jnp.arange(span)
    angles = jnp.concatenate(
        [
            axis_angles(jnp.zeros((span,), jnp.float32) + frame.astype(jnp.float32), RT),
            axis_angles((token // FW).astype(jnp.float32), RH),
            axis_angles((token % FW).astype(jnp.float32), RW),
        ],
        axis=1,
    )
    cosines = jnp.repeat(jnp.cos(angles), 2, axis=1)
    sines = jnp.repeat(jnp.sin(angles), 2, axis=1)

    rings = min(own_heads, 3)
    bf16 = jnp.bfloat16
    whole_frame = pltpu.VMEM((2, frame_tok, width), bf16)
    dma = pltpu.SemaphoreType.DMA
    vmem = pl.BlockSpec(memory_space=pltpu.VMEM)
    anywhere = pl.BlockSpec(memory_space=pl.ANY)
    keys_seen = 3 * frame_tok + slots * BLK
    attended = pl.pallas_call(
        functools.partial(kernel, frames, groups, own_heads, frame_tok, width),
        out_shape=jax.ShapeDtypeStruct((heads, span, width), bf16),
        in_specs=[vmem, vmem, vmem, anywhere, vmem, vmem, vmem, vmem],
        out_specs=anywhere,
        scratch_shapes=[whole_frame] * (3 * own_heads)
        + [pltpu.VMEM((2, slots * BLK, width), bf16)] * own_heads
        + [
            pltpu.VMEM((own_heads, frame_tok, width), bf16),
            pltpu.VMEM((heads, span, width), bf16),
            pltpu.VMEM((heads, span, width), bf16),
            pltpu.VMEM((rings, 2, slots * BLK, width), bf16),
            pltpu.VMEM((own_heads, frame_tok, width), bf16),
            dma((3, own_heads, groups - 1)),
            dma((3, own_heads, groups - 1)),
            dma((3, own_heads)),
            dma((own_heads, 2)),
            dma((own_heads, 2)),
            dma((own_heads, frames - 1)),
            dma((own_heads, frames - 1)),
            dma((own_heads, groups - 1)),
            dma((own_heads, groups - 1)),
            dma((own_heads,)),
        ],
        compiler_params=pltpu.CompilerParams(
            collective_id=0, has_side_effects=True, vmem_limit_bytes=62 * 1024 * 1024
        ),
        cost_estimate=pl.CostEstimate(
            flops=4 * own_heads * frame_tok * keys_seen * width,
            bytes_accessed=8 * heads * span * width,
            transcendentals=own_heads * frame_tok * keys_seen,
        ),
    )(
        picked,
        jnp.transpose(query, (1, 0, 2)),
        jnp.transpose(key, (1, 0, 2)),
        jnp.transpose(value, (1, 0, 2)),
        cosines,
        sines,
        swap_matrix(width),
        bias,
    )
    return jnp.transpose(attended, (1, 0, 2))


def solution(mesh):
    in_specs = (
        P(("tm", "head"), None, None),
        P(("tm", "head"), None, None),
        P(("tm", "head"), None, None),
        P("tm", None),
        P("tm", None),
    )
    out_specs = P(("tm", "head"), None, None)
    return jax.shard_map(shards, mesh=mesh, in_specs=in_specs, out_specs=out_specs, check_vma=False)
```
